256 devices in a mesh: grp: 16 (over y, x), tp: 16 (over z, core).
Axes of the slice: x: 4, y: 4, z: 8, core: 2. Of those that a mesh axis runs over, the one named last changes fastest.
Arguments:
- queries: bfloat16 [512, 128, 576], P(('grp', 'tp')), may hold values from -110 to 110
- latent_cache: bfloat16 [512, 512, 576], P(('grp', 'tp')), may hold values from -6 to 6
- lengths: int32 [512], P(('grp', 'tp')), may hold values from 2 to 512, as said below
- counts: int32 [256], P(('grp', 'tp')), may hold values from 1 to 2, as said below
- residual: bfloat16 [512, 7168], P(None, 'grp'), may hold values from -30 to 30
- value_up: bfloat16 [128, 512, 128], P('tp'), may hold values from -0.75 to 0.75
- out_proj: bfloat16 [16384, 7168], P('tp', 'grp'), may hold values from -0.09375 to 0.09375
- norm_gain: bfloat16 [7168], P('grp'), may hold values from 0.099609375 to 1.8984375
- gate_up: bfloat16 [7168, 2, 18432], P('grp', None, 'tp'), may hold values from -0.0625 to 0.0625
- down_proj: bfloat16 [18432, 7168], P('tp', 'grp'), may hold values from -0.046875 to 0.046875
Outputs:
- mixed: bfloat16 [512, 7168], P('tp', 'grp')
The draws below stay inside these ranges and needn't reach their ends.
Inputs may be any that keep to these rules, and one draw needn't show every extreme that they name: `lengths`: at least 2; exactly 512 for some slot. `counts`: the slots in use on a device are its first ones; exactly 2 on some device.
All inputs are finite; a program needn't handle non-finite values.
Results may differ from the reference program's by a relative error of at most 0.0065.
Values may be sent and summed in bfloat16 or wider, within the bound.
No kernel may reach another device: no remote copies, remote signals or barrier semaphores. Data moves between devices by JAX's collectives and lax.ppermute only.
A program may use at most 64 MiB of HBM per device.

```python
import jax
import jax.numpy as jnp
from jax import lax

D = 7168
FF = 18432
H = 128
KL = 512
RD = 64
VD = 128
QKD = 192
R_DEV = 2
L_MAX = 512
ROWS = 512


def first_keys(key):
    return jnp.clip(jax.random.normal(key, (ROWS, KL + RD), jnp.float32), -6.0, 6.0)


def draw_latent_cache(key, part):
    first = first_keys(key)
    key = jax.random.fold_in(key, 11)
    cache = jnp.clip(jax.random.normal(key, (ROWS, L_MAX, KL + RD), jnp.float32), -6.0, 6.0)
    cache = cache.at[:, 0, :].set(first)
    return cache.astype(jnp.bfloat16)


def draw_queries(key, part):
    key = jax.random.fold_in(key, 7)
    entries = jnp.clip(jax.random.normal(key, (ROWS, H, KL + RD), jnp.float32), -6.0, 6.0)
    return entries.astype(jnp.bfloat16)


def draw_lengths(key, part):
    key = jax.random.fold_in(key, 3)
    ranks = ROWS // R_DEV
    caps = jax.random.randint(jax.random.fold_in(key, 1), (ranks, 1), L_MAX // 8, L_MAX + 1)
    drawn = jax.random.randint(jax.random.fold_in(key, 2), (ranks, R_DEV), 2, caps + 1)
    drawn = drawn.reshape(ROWS)
    longest = jax.random.randint(jax.random.fold_in(key, 4), (), 0, ROWS)
    return drawn.at[longest].set(L_MAX).astype(jnp.int32)


def draw_counts(key, part):
    key = jax.random.fold_in(key, 5)
    ranks = ROWS // R_DEV
    drawn = jax.random.randint(jax.random.fold_in(key, 1), (ranks,), 1, R_DEV + 1)
    fullest = jax.random.randint(jax.random.fold_in(key, 2), (), 0, ranks)
    return drawn.at[fullest].set(R_DEV).astype(jnp.int32)


def draw_residual(key, part):
    key = jax.random.fold_in(key, 9)
    normal_part = jnp.clip(jax.random.normal(key, (ROWS, D), jnp.float32), -6.0, 6.0)
    columns = 0.05 * 10.0 ** (jnp.arange(D, dtype=jnp.float32) / D)
    scales = 10.0 ** jax.random.uniform(jax.random.fold_in(key, 1), (ROWS, 1), jnp.float32)
    return (normal_part * columns[None, :] * scales).astype(jnp.bfloat16)


def block_scale(key, extent, pieces, least, top_value):
    def one(dim, shards_of):
        draws = jax.random.uniform(jax.random.fold_in(jax.random.fold_in(key, 6), dim), (shards_of,), jnp.float32, least / len(pieces), top_value / len(pieces))
        return jnp.repeat(jnp.exp(draws), extent[dim] // shards_of).reshape((-1,) + (1,) * (len(extent) - dim - 1))

    level = one(*pieces[0])
    for cut in pieces[1:]:
        level = level * one(*cut)
    return level


def centred(own_key, shape, spread, bound, pieces=(), kind=jnp.bfloat16):
    factor_of = block_scale(own_key, shape, pieces, -0.22, 0.18) if pieces else 1.0
    values = jax.random.normal(own_key, shape, jnp.float32) * spread * factor_of
    return jnp.minimum(jnp.maximum(values, -bound), bound).astype(kind)


def setup_inputs(seed: int = 0) -> dict:
    streams_of = jax.random.split(jax.random.key(seed), 11)
    queries = draw_queries(jax.random.fold_in(streams_of[10], 71), 0)
    latent_cache = draw_latent_cache(jax.random.fold_in(streams_of[10], 71), 0)
    lengths = draw_lengths(jax.random.fold_in(streams_of[10], 71), 0)
    counts = draw_counts(jax.random.fold_in(streams_of[10], 71), 0)
    residual = draw_residual(jax.random.fold_in(streams_of[10], 71), 0)
    value_up = centred(streams_of[5], (H, KL, VD), 64 ** -0.5, 0.75, ((0, 16),))
    out_proj = centred(streams_of[6], (H * VD, D), (H * VD // 4) ** -0.5, 0.09375, ((0, 16), (1, 16)))
    norm_gain = jnp.clip(1.0 + 0.18 * jax.random.normal(streams_of[7], (D,), jnp.float32), 0.099609375, 1.8984375).astype(jnp.bfloat16)
    gate_up = centred(streams_of[8], (D, 2, FF), D ** -0.5, 0.0625, ((0, 16), (2, 16)))
    down_proj = centred(streams_of[9], (FF, D), FF ** -0.5, 0.046875, ((0, 16), (1, 16)))
    return dict(queries=queries, latent_cache=latent_cache, lengths=lengths, counts=counts, residual=residual, value_up=value_up, out_proj=out_proj, norm_gain=norm_gain, gate_up=gate_up, down_proj=down_proj)


def attend_row(query, cache, length):
    scores = jnp.dot(query.astype(jnp.float32), cache.astype(jnp.float32).T, preferred_element_type=jnp.float32) * QKD ** (-0.5)
    place = lax.broadcasted_iota(jnp.int32, scores.shape, 1)
    scores = jnp.where(place < length, scores, -jnp.inf)
    expo = jnp.exp(scores - lax.optimization_barrier(jnp.max(scores, axis=1, keepdims=True)))
    totals = lax.optimization_barrier(jnp.sum(expo, axis=1, keepdims=True))
    probs = lax.optimization_barrier(expo.astype(jnp.bfloat16))
    summed = jnp.dot(probs.astype(jnp.float32), cache[:, :KL].astype(jnp.float32), preferred_element_type=jnp.float32)
    return (summed / totals).astype(jnp.bfloat16)

def reference(queries, latent_cache, lengths, counts, residual, value_up, out_proj, norm_gain, gate_up, down_proj):
    attended = lax.map(lambda item: attend_row(item[0], item[1], item[2]), (queries, latent_cache, lengths))
    slot_ids = lax.broadcasted_iota(jnp.int32, (ROWS,), 0)
    owner_counts = jnp.repeat(counts, R_DEV)
    in_use = slot_ids % R_DEV < owner_counts
    attended = jnp.where(in_use[:, None, None], attended, jnp.zeros_like(attended))
    values = jnp.einsum('rhk,hkd->rhd', attended.astype(jnp.float32), value_up.astype(jnp.float32)).astype(jnp.bfloat16)
    projected = jnp.dot(values.reshape(ROWS, H * VD), out_proj, preferred_element_type=jnp.float32)
    combined = residual.astype(jnp.float32) + projected
    factor = lax.rsqrt(lax.optimization_barrier(jnp.mean(combined * combined, axis=1, keepdims=True)) + 1e-06)
    normed = (combined * factor * norm_gain.astype(jnp.float32)).astype(jnp.bfloat16)
    gate = jnp.dot(normed, gate_up[:, 0, :], preferred_element_type=jnp.float32)
    up = jnp.dot(normed, gate_up[:, 1, :], preferred_element_type=jnp.float32)
    hidden = (jax.nn.silu(gate) * up).astype(jnp.bfloat16)
    mixed = combined + jnp.dot(hidden, down_proj, preferred_element_type=jnp.float32)
    return mixed.astype(jnp.bfloat16)
```

```python
import jax
import jax.numpy as jnp
from jax import lax
from jax.sharding import Mesh, PartitionSpec as P

D = 7168
KL = 512
QKD = 192
GRP = ("y", "x")
TP = ("z", "c")
BF = jnp.bfloat16
F32 = jnp.float32


def exchange(parts, axes):
    return lax.all_to_all(parts, axes, split_axis=0, concat_axis=0, tiled=False)


def gather(block, axes, n):
    return exchange(jnp.broadcast_to(block[None], (n,) + block.shape), axes)


def attend(queries, cache, lengths):
    scores = jnp.einsum("rhk,rlk->rhl", queries, cache, preferred_element_type=F32)
    scores = scores * QKD ** (-0.5)
    place = lax.broadcasted_iota(jnp.int32, (1, 1, cache.shape[1]), 2)
    scores = jnp.where(place < lengths[:, None, None], scores, -jnp.inf)
    expo = jnp.exp(scores - jnp.max(scores, axis=2, keepdims=True))
    totals = jnp.sum(expo, axis=2, keepdims=True)
    summed = jnp.einsum(
        "rhl,rlk->rhk", expo.astype(BF), cache[:, :, :KL], preferred_element_type=F32
    )
    return summed / totals


def split_sum(x):
    high = x.astype(BF)
    return high, (x - high.astype(F32)).astype(BF)


def local(
    queries,
    latent_cache,
    lengths,
    counts,
    residual,
    value_up,
    out_proj,
    norm_gain,
    gate_up,
    down_proj,
):
    slots = queries.shape[0]
    heads = value_up.shape[0]
    n = 16
    in_use = lax.broadcasted_iota(jnp.int32, (slots,), 0) < counts[0]
    attended = jnp.where(
        in_use[:, None, None], attend(queries, latent_cache, lengths), 0.0
    ).astype(BF)
    received = lax.all_to_all(attended, TP, split_axis=1, concat_axis=0, tiled=True)
    values = jnp.einsum(
        "rhk,hkd->rhd", received, value_up, preferred_element_type=F32
    ).astype(BF)
    rows = values.shape[0]
    values = gather(values.reshape(rows, -1), GRP, n).reshape(n * rows, -1)
    partial = jnp.dot(values, out_proj, preferred_element_type=F32).astype(BF)
    share = partial.shape[0] // n
    pieces = exchange(partial.reshape(n, share, -1), TP)
    projected = jnp.sum(pieces.astype(F32), axis=0)
    offset = lax.axis_index(TP) * share
    mine = lax.dynamic_slice_in_dim(residual, offset, share, 0)
    combined = mine.astype(F32) + projected
    high, low = split_sum(jnp.sum(combined * combined, axis=1, keepdims=True))
    scaled = (combined * norm_gain.astype(F32)).astype(BF)
    feats = scaled.shape[1]
    packed = jnp.concatenate(
        [scaled, high, low, jnp.zeros((share, 512 - feats - 2), BF)], axis=1
    )
    packed = gather(packed, TP, n).reshape(n * share, 512)
    units = gate_up.shape[2]
    joined = gate_up.reshape(feats, 2 * units)
    terms = jnp.dot(packed[:, :feats], joined, preferred_element_type=F32).astype(BF)
    terms = jnp.concatenate([terms, packed[:, feats : feats + 2], jnp.zeros((n * share, 126), BF)], axis=1)
    summed = jnp.sum(
        exchange(terms.reshape(n, share, -1), GRP).astype(F32), axis=0
    )
    squares = summed[:, 2 * units] + summed[:, 2 * units + 1]
    factor = lax.rsqrt(squares / D + 1e-06)[:, None]
    gate = summed[:, :units] * factor
    up = summed[:, units : 2 * units] * factor
    hidden = (jax.nn.silu(gate) * up).astype(BF)
    hidden = gather(hidden, GRP, n).reshape(n * share, units)
    last = jnp.dot(hidden, down_proj, preferred_element_type=F32).astype(BF)
    last = exchange(last.reshape(n, share, -1), TP)
    return (combined + jnp.sum(last.astype(F32), axis=0)).astype(BF)


def solution(mesh):
    inner = Mesh(mesh.devices.reshape(4, 4, 8, 2), GRP + TP)
    every = GRP + TP
    placed = (
        P(every, None, None),
        P(every, None, None),
        P(every),
        P(every),
        P(None, GRP),
        P(TP, None, None),
        P(TP, GRP),
        P(GRP),
        P(GRP, None, TP),
        P(TP, GRP),
    )
    return jax.shard_map(
        local, mesh=inner, in_specs=placed, out_specs=P(TP, GRP), check_vma=False
    )
```

```python
import jax
import jax.numpy as jnp
from jax import lax
from jax.sharding import Mesh, PartitionSpec as P

D = 7168
KL = 512
QKD = 192
GRP = ("y", "x")
TP = ("z", "c")
BF = jnp.bfloat16
F32 = jnp.float32


def exchange(parts, axes):
    return lax.all_to_all(parts, axes, split_axis=0, concat_axis=0, tiled=False)


def gather(block, axes, n):
    return exchange(jnp.broadcast_to(block[None], (n,) + block.shape), axes)


def attend(queries, cache, lengths):
    scores = jnp.einsum("rhk,rlk->rhl", queries, cache, preferred_element_type=F32)
    scores = scores * QKD ** (-0.5)
    place = lax.broadcasted_iota(jnp.int32, (1, 1, cache.shape[1]), 2)
    scores = jnp.where(place < lengths[:, None, None], scores, -jnp.inf)
    expo = jnp.exp(scores - jnp.max(scores, axis=2, keepdims=True))
    totals = jnp.sum(expo, axis=2, keepdims=True)
    summed = jnp.einsum(
        "rhl,rlk->rhk", expo.astype(BF), cache[:, :, :KL], preferred_element_type=F32
    )
    return summed / totals


def split_sum(x):
    high = x.astype(BF)
    return high, (x - high.astype(F32)).astype(BF)


def local(
    queries,
    latent_cache,
    lengths,
    counts,
    residual,
    value_up,
    out_proj,
    norm_gain,
    gate_up,
    down_proj,
):
    slots = queries.shape[0]
    core = lax.axis_index("c")
    value_up, out_proj, gate_up, down_proj = [
        (w, lax.ppermute(w, "c", [(0, 1), (1, 0)]))
        for w in (value_up, out_proj, gate_up, down_proj)
    ]
    in_use = lax.broadcasted_iota(jnp.int32, (slots,), 0) < counts[0]
    attended = jnp.where(
        in_use[:, None, None], attend(queries, latent_cache, lengths), 0.0
    ).astype(BF)
    paired = attended.reshape(slots, 8, 2, 8, KL)
    paired = jnp.where(core == 0, paired, paired[:, :, ::-1])
    paired = jnp.transpose(paired, (1, 0, 2, 3, 4))
    received = exchange(paired, "z").reshape(8 * slots, 2, 8, KL)
    values = [
        jnp.einsum(
            "rhk,hkd->rhd", received[:, i], value_up[i], preferred_element_type=F32
        )
        .astype(BF)
        .reshape(8 * slots, -1)
        for i in range(2)
    ]
    values = gather(jnp.concatenate(values, axis=1), GRP, 16).reshape(256, -1)
    depth = out_proj[0].shape[0]
    partial = sum(
        jnp.dot(
            values[:, i * depth : (i + 1) * depth],
            out_proj[i],
            preferred_element_type=F32,
        )
        for i in range(2)
    ).astype(BF)
    feats = partial.shape[1]
    pieces = exchange(partial.reshape(16, 16, feats), TP)
    projected = jnp.sum(pieces.astype(F32).reshape(8, 2, 8, 2, feats), axis=0)
    projected = jnp.transpose(projected, (1, 0, 2, 3)).reshape(32, feats)
    offset = lax.axis_index(TP) * 32
    mine = lax.dynamic_slice_in_dim(residual, offset, 32, 0)
    combined = mine.astype(F32) + projected
    high, low = split_sum(jnp.sum(combined * combined, axis=1, keepdims=True))
    scaled = (combined * norm_gain.astype(F32)).astype(BF)
    packed = jnp.concatenate(
        [scaled, high, low, jnp.zeros((32, 512 - feats - 2), BF)], axis=1
    )
    packed = gather(packed, "z", 8).reshape(256, 512)
    units = gate_up[0].shape[2]
    terms = [
        jnp.dot(
            packed[:, :feats], w.reshape(feats, 2 * units), preferred_element_type=F32
        ).astype(BF)
        for w in gate_up
    ]
    terms = jnp.concatenate(
        terms + [packed[:, feats : feats + 2], jnp.zeros((256, 126), BF)], axis=1
    )
    summed = jnp.sum(exchange(terms.reshape(16, 16, -1), GRP).astype(F32), axis=0)
    squares = summed[:, 4 * units] + summed[:, 4 * units + 1]
    factor = lax.rsqrt(squares / D + 1e-06)[:, None]
    hidden = []
    for i in range(2):
        gate = summed[:, 2 * i * units : (2 * i + 1) * units] * factor
        up = summed[:, (2 * i + 1) * units : (2 * i + 2) * units] * factor
        hidden.append((jax.nn.silu(gate) * up).astype(BF))
    hidden = gather(jnp.concatenate(hidden, axis=1), GRP, 16).reshape(256, 2 * units)
    last = sum(
        jnp.dot(
            hidden[:, i * units : (i + 1) * units],
            down_proj[i],
            preferred_element_type=F32,
        )
        for i in range(2)
    ).astype(BF)
    last = exchange(last.reshape(8, 32, feats), "z")
    return (combined + jnp.sum(last.astype(F32), axis=0)).astype(BF)


def solution(mesh):
    inner = Mesh(mesh.devices.reshape(4, 4, 8, 2), GRP + TP)
    every = GRP + TP
    placed = (
        P(every, None, None),
        P(every, None, None),
        P(every),
        P(every),
        P(None, GRP),
        P(TP, None, None),
        P(TP, GRP),
        P(GRP),
        P(GRP, None, TP),
        P(TP, GRP),
    )
    return jax.shard_map(
        local, mesh=inner, in_specs=placed, out_specs=P(TP, GRP), check_vma=False
    )
```

```python
import jax
import jax.numpy as jnp
from jax import lax
from jax.experimental import pallas as pl
from jax.experimental.pallas import tpu as pltpu
from jax.sharding import Mesh, PartitionSpec as P

D = 7168
KL = 512
QKD = 192
GRP = ("y", "x")
TP = ("z", "c")
BF = jnp.bfloat16
F32 = jnp.float32


def exchange(parts, axes):
    return lax.all_to_all(parts, axes, split_axis=0, concat_axis=0, tiled=False)


def call(body, shapes, *args, smem=0, limit=40):
    return pl.pallas_call(
        body,
        out_shape=shapes,
        in_specs=[
            pl.BlockSpec(memory_space=pltpu.SMEM if i < smem else pltpu.VMEM)
            for i in range(len(args))
        ],
        compiler_params=pltpu.CompilerParams(vmem_limit_bytes=limit * 2**20),
    )(*args)


def iota(shape, dim):
    return lax.broadcasted_iota(jnp.int32, shape, dim)


def mm(a, b):
    return jnp.dot(a, b, preferred_element_type=F32)


def mm_t(a, b):
    return lax.dot_general(a, b, (((1,), (1,)), ((), ())), preferred_element_type=F32)


def attend_body(lengths, counts, q_ref, c_ref, o_ref):
    for slot in range(2):
        query = q_ref[slot].T
        scores = mm(query, c_ref[slot]) * QKD ** (-0.5)
        scores = jnp.where(iota(scores.shape, 1) < lengths[slot], scores, -jnp.inf)
        expo = jnp.exp(scores - jnp.max(scores, axis=1, keepdims=True))
        scale = 1.0 / jnp.sum(expo, axis=1, keepdims=True)
        summed = mm_t(expo.astype(BF), c_ref[slot, :KL, :])
        summed = jnp.where(slot < counts[0], summed * scale, 0.0)
        o_ref[:, slot] = summed.astype(BF).reshape(8, 16, KL)


def value_body(core, x_ref, own_ref, other_ref, o_ref):
    x = x_ref[...]
    pick = ((iota((256, 256), 0) & 15) == (iota((256, 256), 1) >> 4)).astype(BF)
    head = (iota((256, 256), 0) & 15) - (iota((256, 256), 1) >> 7)
    for i, w_ref in enumerate((own_ref, other_ref)):
        first = 8 * (core[0] if i == 0 else 1 - core[0])
        for j in range(0, 8, 2):
            w = jnp.concatenate([w_ref[j], w_ref[j + 1]], axis=1)
            full = jnp.where(head == first + j, mm(x, w), 0.0).astype(BF)
            at = i * 1024 + j * 128
            o_ref[:, at : at + 256] = mm(pick, full).astype(BF)


def out_body(v_ref, own_ref, other_ref, o_ref):
    depth = own_ref.shape[1]
    total = mm_t(v_ref[:, :depth], own_ref[...])
    total = total + mm_t(v_ref[:, depth:], other_ref[...])
    o_ref[...] = total.astype(BF)


def mix_body(p_ref, mine_ref, gain_ref, c_ref, o_ref):
    k = iota((32, 256), 1)
    place = ((k >> 1) & 7) * 4 + ((k >> 4) & 1) * 2 + (k & 1)
    pick = (iota((32, 256), 0) == place).astype(BF)
    combined = mine_ref[...].astype(F32) + mm(pick, p_ref[...])
    c_ref[...] = combined
    squares = jnp.sum(combined * combined, axis=1, keepdims=True)
    high = squares.astype(BF).astype(F32)
    lane = iota((32, 512), 1)
    extra = jnp.where(lane == 448, high, jnp.where(lane == 449, squares - high, 0.0))
    extra = extra.astype(BF)
    scaled = (combined * gain_ref[...].astype(F32)).astype(BF)
    for z in range(8):
        o_ref[z] = extra
        o_ref[z, :, :448] = scaled


def units_body(x_ref, own_ref, other_ref, o_ref):
    x = x_ref[:, :448]
    width = own_ref.shape[1]
    step = 768
    for i, w_ref in enumerate((own_ref, other_ref)):
        for j in range(0, width, step):
            at = i * width + j
            o_ref[:, at : at + step] = mm(x, w_ref[:, j : j + step]).astype(BF)
    o_ref[:, 2 * width :] = x_ref[:, 384:]


def gate_body(p_ref, o_ref):
    units = o_ref.shape[2] // 2
    tail = jnp.sum(p_ref[:, :, 4 * units :].astype(F32), axis=0)
    lane = iota(tail.shape, 1)
    tail = jnp.where((lane == 64) | (lane == 65), tail, 0.0)
    factor = lax.rsqrt(jnp.sum(tail, axis=1, keepdims=True) / D + 1e-06)
    step = 384
    for i in range(2):
        for j in range(0, units, step):
            at = 2 * i * units + j
            gate = jnp.sum(p_ref[:, :, at : at + step].astype(F32), axis=0) * factor
            at = at + units
            up = jnp.sum(p_ref[:, :, at : at + step].astype(F32), axis=0) * factor
            hidden = (gate / (1.0 + jnp.exp(-gate)) * up).astype(BF)
            at = i * units + j
            for r in range(16):
                o_ref[r, :, at : at + step] = hidden


def local(
    queries,
    latent_cache,
    lengths,
    counts,
    residual,
    value_up,
    out_proj,
    norm_gain,
    gate_up,
    down_proj,
):
    shape = jax.ShapeDtypeStruct
    core = lax.axis_index("c").reshape(1)
    out_proj = out_proj.T
    down_proj = down_proj.T
    value_up, out_proj, gate_up, down_proj = [
        (w, lax.ppermute(w, "c", [(0, 1), (1, 0)]))
        for w in (value_up, out_proj, gate_up, down_proj)
    ]
    attended = call(
        attend_body,
        shape((8, 2, 16, KL), BF),
        lengths,
        counts,
        jnp.swapaxes(queries, 1, 2),
        jnp.swapaxes(latent_cache, 1, 2),
        smem=2,
    )
    received = exchange(attended, "z").reshape(256, KL)
    values = call(value_body, shape((256, 2048), BF), core, received, *value_up, smem=1)
    values = exchange(values.reshape(16, 16, 2048), GRP).reshape(256, 2048)
    feats = residual.shape[1]
    partial = call(out_body, shape((256, feats), BF), values, *out_proj)
    pieces = exchange(partial.reshape(16, 16, feats), TP).reshape(256, feats)
    mine = lax.dynamic_slice_in_dim(residual, lax.axis_index(TP) * 32, 32, 0)
    combined, packed = call(
        mix_body,
        (shape((32, feats), F32), shape((8, 32, 512), BF)),
        pieces,
        mine,
        norm_gain.reshape(1, feats),
    )
    packed = exchange(packed, "z").reshape(256, 512)
    units = gate_up[0].shape[2]
    terms = call(
        units_body,
        shape((256, 4 * units + 128), BF),
        packed,
        *[w.reshape(feats, 2 * units) for w in gate_up],
    )
    terms = exchange(terms.reshape(16, 16, -1), GRP)
    hidden = call(gate_body, shape((16, 16, 2 * units), BF), terms)
    hidden = exchange(hidden, GRP).reshape(256, 2 * units)
    last = call(out_body, shape((256, feats), BF), hidden, *down_proj)
    last = exchange(last.reshape(8, 32, feats), "z")
    return (combined + jnp.sum(last.astype(F32), axis=0)).astype(BF)


def solution(mesh):
    inner = Mesh(mesh.devices.reshape(4, 4, 8, 2), GRP + TP)
    every = GRP + TP
    placed = (
        P(every, None, None),
        P(every, None, None),
        P(every),
        P(every),
        P(None, GRP),
        P(TP, None, None),
        P(TP, GRP),
        P(GRP),
        P(GRP, None, TP),
        P(TP, GRP),
    )
    return jax.shard_map(
        local, mesh=inner, in_specs=placed, out_specs=P(TP, GRP), check_vma=False
    )
```

```python
import jax
import jax.numpy as jnp
from jax import lax
from jax.experimental import pallas as pl
from jax.experimental.pallas import tpu as pltpu
from jax.sharding import Mesh, PartitionSpec as P

D = 7168
KL = 512
QKD = 192
GRP = ("y", "x")
TP = ("z", "c")
XYC = ("y", "x", "c")
LINES_X = [[[8 * y + 2 * x + c for x in range(4)] for y in range(4)] for c in range(2)]
LINES_Y = [[[8 * y + 2 * x + c for y in range(4)] for x in range(4)] for c in range(2)]
FIRST = LINES_X[0] + LINES_Y[1]
SECOND = LINES_Y[0] + LINES_X[1]
BF = jnp.bfloat16
F32 = jnp.float32


def exchange(parts, axes, groups=None):
    return lax.all_to_all(
        parts, axes, split_axis=0, concat_axis=0, axis_index_groups=groups
    )


def call(body, shapes, *args, smem=0, any_space=0, scratch=(), limit=8):
    spaces = [pltpu.SMEM] * smem + [pltpu.HBM] * any_space
    spaces = spaces + [pltpu.VMEM] * (len(args) - len(spaces))
    return pl.pallas_call(
        body,
        out_shape=shapes,
        in_specs=[pl.BlockSpec(memory_space=space) for space in spaces],
        scratch_shapes=scratch,
        compiler_params=pltpu.CompilerParams(vmem_limit_bytes=limit * 2**20),
    )(*args)


def iota(shape, dim):
    return lax.broadcasted_iota(jnp.int32, shape, dim)


def mm(a, b):
    return jnp.dot(a, b, preferred_element_type=F32)


def mm_t(a, b):
    return lax.dot_general(a, b, (((1,), (1,)), ((), ())), preferred_element_type=F32)


def attend_body(len_hbm, cnt_hbm, q_hbm, c_hbm, o_ref, lengths, counts, q_ref, c_ref, sems):
    copies = [
        pltpu.make_async_copy(len_hbm, lengths, sems.at[0]),
        pltpu.make_async_copy(cnt_hbm, counts, sems.at[1]),
    ]
    for slot in range(2):
        copies.append(
            pltpu.make_async_copy(q_hbm.at[slot], q_ref.at[slot], sems.at[2 + 2 * slot])
        )
        copies.append(
            pltpu.make_async_copy(c_hbm.at[slot], c_ref.at[slot], sems.at[3 + 2 * slot])
        )
    for copy in copies:
        copy.start()
    copies[0].wait()
    copies[1].wait()
    for slot in range(2):
        copies[2 + 2 * slot].wait()
        query = q_ref[slot].T
        copies[3 + 2 * slot].wait()
        scores = mm(query, c_ref[slot]) * QKD ** (-0.5)
        scores = jnp.where(iota(scores.shape, 1) < lengths[slot], scores, -jnp.inf)
        expo = jnp.exp(scores - jnp.max(scores, axis=1, keepdims=True))
        scale = 1.0 / jnp.sum(expo, axis=1, keepdims=True)
        summed = mm_t(expo.astype(BF), c_ref[slot, :KL, :])
        summed = jnp.where(slot < counts[0], summed * scale, 0.0)
        o_ref[:, slot] = summed.astype(BF).reshape(8, 16, KL)


def value_body(core, x_ref, own_ref, other_ref, o_ref):
    at = iota((256, 256), 0)
    source = (at & 15) * 16 + ((at >> 4) ^ (8 * core[0]))
    pick = (iota((256, 256), 1) == source).astype(BF)
    x = mm(pick, x_ref[...]).astype(BF)
    for i, w_ref in enumerate((own_ref, other_ref)):
        for h in range(8):
            k = 8 * i + h
            value = mm(x[16 * k : 16 * k + 16], w_ref[h]).astype(BF)
            for r in range(16):
                o_ref[16 * r : 16 * r + 16, 128 * k : 128 * k + 128] = value


def out_body(v_ref, own_ref, other_ref, o_ref):
    depth = own_ref.shape[1]
    total = mm_t(v_ref[:, :depth], own_ref[...])
    total = total + mm_t(v_ref[:, depth:], other_ref[...])
    o_ref[...] = total.astype(BF)


def mix_body(p_ref, mine_ref, gain_ref, c_ref, o_ref):
    k = iota((32, 256), 1)
    place = ((k >> 1) & 7) * 4 + ((k >> 4) & 1) * 2 + (k & 1)
    pick = (iota((32, 256), 0) == place).astype(BF)
    combined = mine_ref[...].astype(F32) + mm(pick, p_ref[...])
    c_ref[...] = combined
    squares = jnp.sum(combined * combined, axis=1, keepdims=True)
    high = squares.astype(BF).astype(F32)
    lane = iota((32, 512), 1)
    extra = jnp.where(lane == 448, high, jnp.where(lane == 449, squares - high, 0.0))
    extra = extra.astype(BF)
    scaled = (combined * gain_ref[...].astype(F32)).astype(BF)
    for z in range(8):
        o_ref[z] = extra
        o_ref[z, :, :448] = scaled


def units_body(core, x_ref, own_ref, other_ref, o_ref, rows_ref):
    for i in range(4):
        for j in range(4):
            block = jnp.where(core[0] == 0, 4 * j + i, 4 * i + j)
            at = pl.multiple_of(block * 16, 16)
            to = 16 * (4 * i + j)
            rows_ref[to : to + 16] = x_ref[pl.ds(at, 16)]
    x = rows_ref[:, :448]
    width = own_ref.shape[1]
    step = 768
    for i, w_ref in enumerate((own_ref, other_ref)):
        for j in range(0, width, step):
            at = i * width + j
            o_ref[:, at : at + step] = mm(x, w_ref[:, j : j + step]).astype(BF)
    o_ref[:, 2 * width :] = rows_ref[:, 384:]


def half_body(p_ref, o_ref):
    width = o_ref.shape[1] - 128
    step = width // 6
    for j in range(0, width, step):
        part = p_ref[:, :, j : j + step].astype(F32)
        o_ref[:, j : j + step] = jnp.sum(part, axis=0).astype(BF)
    tail = jnp.sum(p_ref[:, :, width:].astype(F32), axis=0)
    lane = iota(tail.shape, 1)
    tail = jnp.where((lane == 64) | (lane == 65), tail, 0.0)
    squares = jnp.sum(tail, axis=1, keepdims=True)
    high = squares.astype(BF).astype(F32)
    tail = jnp.where(lane == 64, high, jnp.where(lane == 65, squares - high, 0.0))
    o_ref[:, width:] = tail.astype(BF)


def gate_body(p_ref, o_ref):
    units = o_ref.shape[2] // 2
    tail = jnp.sum(p_ref[:, :, 4 * units :].astype(F32), axis=0)
    lane = iota(tail.shape, 1)
    tail = jnp.where((lane == 64) | (lane == 65), tail, 0.0)
    factor = lax.rsqrt(jnp.sum(tail, axis=1, keepdims=True) / D + 1e-06)
    step = 384
    for i in range(2):
        for j in range(0, units, step):
            at = 2 * i * units + j
            gate = jnp.sum(p_ref[:, :, at : at + step].astype(F32), axis=0) * factor
            at = at + units
            up = jnp.sum(p_ref[:, :, at : at + step].astype(F32), axis=0) * factor
            hidden = (gate / (1.0 + jnp.exp(-gate)) * up).astype(BF)
            at = i * units + j
            for r in range(16):
                o_ref[r, :, at : at + step] = hidden


def local(
    queries,
    latent_cache,
    lengths,
    counts,
    residual,
    value_up,
    out_proj,
    norm_gain,
    gate_up,
    down_proj,
):
    shape = jax.ShapeDtypeStruct
    core = lax.axis_index("c").reshape(1)
    out_proj = out_proj.T
    down_proj = down_proj.T
    value_up, out_proj, gate_up, down_proj = [
        (w, lax.ppermute(w, "c", [(0, 1), (1, 0)]))
        for w in (value_up, out_proj, gate_up, down_proj)
    ]
    attended = call(
        attend_body,
        shape((8, 2, 16, KL), BF),
        lengths,
        counts,
        jnp.swapaxes(queries, 1, 2),
        jnp.swapaxes(latent_cache, 1, 2),
        any_space=4,
        scratch=[
            pltpu.SMEM((2,), jnp.int32),
            pltpu.SMEM((1,), jnp.int32),
            pltpu.VMEM((2, 576, 128), BF),
            pltpu.VMEM((2, 576, 512), BF),
            pltpu.SemaphoreType.DMA((6,)),
        ],
        limit=60,
    )
    received = exchange(attended, "z").reshape(256, KL)
    values = call(value_body, shape((256, 2048), BF), core, received, *value_up, smem=1)
    values = exchange(values.reshape(16, 16, 2048), GRP).reshape(256, 2048)
    feats = residual.shape[1]
    partial = call(out_body, shape((256, feats), BF), values, *out_proj)
    pieces = exchange(partial.reshape(16, 16, feats), TP).reshape(256, feats)
    mine = lax.dynamic_slice_in_dim(residual, lax.axis_index(TP) * 32, 32, 0)
    combined, packed = call(
        mix_body,
        (shape((32, feats), F32), shape((8, 32, 512), BF)),
        pieces,
        mine,
        norm_gain.reshape(1, feats),
    )
    packed = exchange(packed, "z").reshape(256, 512)
    units = gate_up[0].shape[2]
    terms = call(
        units_body,
        shape((256, 4 * units + 128), BF),
        core,
        packed,
        *[w.reshape(feats, 2 * units) for w in gate_up],
        smem=1,
        scratch=[pltpu.VMEM((256, 512), BF)],
    )
    terms = exchange(terms.reshape(4, 64, -1), XYC, FIRST)
    terms = call(half_body, shape(terms.shape[1:], BF), terms)
    terms = exchange(terms.reshape(4, 16, -1), XYC, SECOND)
    hidden = call(gate_body, shape((16, 16, 2 * units), BF), terms)
    hidden = exchange(hidden, GRP).reshape(256, 2 * units)
    last = call(out_body, shape((256, feats), BF), hidden, *down_proj)
    last = exchange(last.reshape(8, 32, feats), "z")
    return (combined + jnp.sum(last.astype(F32), axis=0)).astype(BF)


def solution(mesh):
    inner = Mesh(mesh.devices.reshape(4, 4, 8, 2), GRP + TP)
    every = GRP + TP
    placed = (
        P(every, None, None),
        P(every, None, None),
        P(every),
        P(every),
        P(None, GRP),
        P(TP, None, None),
        P(TP, GRP),
        P(GRP),
        P(GRP, None, TP),
        P(TP, GRP),
    )
    return jax.shard_map(
        local, mesh=inner, in_specs=placed, out_specs=P(TP, GRP), check_vma=False
    )
```

```python
import jax
import jax.numpy as jnp
from jax import lax
from jax.experimental import pallas as pl
from jax.experimental.pallas import tpu as pltpu
from jax.sharding import Mesh, PartitionSpec as P

D = 7168
KL = 512
QKD = 192
GRP = ("y", "x")
TP = ("z", "c")
XYC = ("y", "x", "c")
LINES_X = [[[8 * y + 2 * x + c for x in range(4)] for y in range(4)] for c in range(2)]
LINES_Y = [[[8 * y + 2 * x + c for y in range(4)] for x in range(4)] for c in range(2)]
FIRST = LINES_X[0] + LINES_Y[1]
SECOND = LINES_Y[0] + LINES_X[1]
BF = jnp.bfloat16
F32 = jnp.float32


def exchange(parts, axes, groups=None):
    return lax.all_to_all(
        parts, axes, split_axis=0, concat_axis=0, axis_index_groups=groups
    )


def call(body, shapes, *args, smem=0, any_space=0, scratch=(), limit=8, flops=500000000):
    arrays = jax.tree.leaves((args, shapes))
    size = sum(a.size * a.dtype.itemsize for a in arrays)
    cost = pl.CostEstimate(flops=flops, bytes_accessed=size, transcendentals=0)
    spaces = [pltpu.SMEM] * smem + [pltpu.HBM] * any_space
    spaces = spaces + [pltpu.VMEM] * (len(args) - len(spaces))
    return pl.pallas_call(
        body,
        out_shape=shapes,
        in_specs=[pl.BlockSpec(memory_space=space) for space in spaces],
        scratch_shapes=scratch,
        cost_estimate=cost,
        compiler_params=pltpu.CompilerParams(vmem_limit_bytes=limit * 2**20),
    )(*args)


def iota(shape, dim):
    return lax.broadcasted_iota(jnp.int32, shape, dim)


def mm(a, b):
    return jnp.dot(a, b, preferred_element_type=F32)


def mm_t(a, b):
    return lax.dot_general(a, b, (((1,), (1,)), ((), ())), preferred_element_type=F32)


def attend_body(len_hbm, cnt_hbm, q_hbm, c_hbm, o_ref, lengths, counts, q_ref, c_ref, sems):
    copies = [
        pltpu.make_async_copy(len_hbm, lengths, sems.at[0]),
        pltpu.make_async_copy(cnt_hbm, counts, sems.at[1]),
    ]
    for slot in range(2):
        copies.append(
            pltpu.make_async_copy(q_hbm.at[slot], q_ref.at[slot], sems.at[2 + 2 * slot])
        )
        copies.append(
            pltpu.make_async_copy(c_hbm.at[slot], c_ref.at[slot], sems.at[3 + 2 * slot])
        )
    for copy in copies:
        copy.start()
    copies[0].wait()
    copies[1].wait()
    for slot in range(2):
        copies[2 + 2 * slot].wait()
        query = q_ref[slot].T
        copies[3 + 2 * slot].wait()
        scores = mm(query, c_ref[slot]) * QKD ** (-0.5)
        scores = jnp.where(iota(scores.shape, 1) < lengths[slot], scores, -jnp.inf)
        expo = jnp.exp(scores - jnp.max(scores, axis=1, keepdims=True))
        scale = 1.0 / jnp.sum(expo, axis=1, keepdims=True)
        summed = mm_t(expo.astype(BF), c_ref[slot, :KL, :])
        summed = jnp.where(slot < counts[0], summed * scale, 0.0)
        o_ref[:, slot] = summed.astype(BF).reshape(8, 16, KL)


def value_body(core, x_ref, own_ref, other_ref, o_ref):
    at = iota((256, 256), 0)
    source = (at & 15) * 16 + ((at >> 4) ^ (8 * core[0]))
    pick = (iota((256, 256), 1) == source).astype(BF)
    x = mm(pick, x_ref[...]).astype(BF)
    for i, w_ref in enumerate((own_ref, other_ref)):
        for h in range(8):
            k = 8 * i + h
            value = mm(x[16 * k : 16 * k + 16], w_ref[h]).astype(BF)
            for r in range(16):
                o_ref[16 * r : 16 * r + 16, 128 * k : 128 * k + 128] = value


def out_body(v_ref, own_ref, other_ref, o_ref):
    depth = own_ref.shape[1]
    total = mm_t(v_ref[:, :depth], own_ref[...])
    total = total + mm_t(v_ref[:, depth:], other_ref[...])
    o_ref[...] = total.astype(BF)


def mix_body(p_ref, mine_ref, gain_ref, c_ref, o_ref):
    k = iota((32, 256), 1)
    place = ((k >> 1) & 7) * 4 + ((k >> 4) & 1) * 2 + (k & 1)
    pick = (iota((32, 256), 0) == place).astype(BF)
    combined = mine_ref[...].astype(F32) + mm(pick, p_ref[...])
    c_ref[...] = combined
    squares = jnp.sum(combined * combined, axis=1, keepdims=True)
    high = squares.astype(BF).astype(F32)
    lane = iota((32, 512), 1)
    extra = jnp.where(lane == 448, high, jnp.where(lane == 449, squares - high, 0.0))
    extra = extra.astype(BF)
    scaled = (combined * gain_ref[...].astype(F32)).astype(BF)
    for z in range(8):
        o_ref[z] = extra
        o_ref[z, :, :448] = scaled


def units_body(core, x_ref, own_ref, other_ref, o_ref, rows_ref):
    for i in range(4):
        for j in range(4):
            block = jnp.where(core[0] == 0, 4 * j + i, 4 * i + j)
            at = pl.multiple_of(block * 16, 16)
            to = 16 * (4 * i + j)
            rows_ref[to : to + 16] = x_ref[pl.ds(at, 16)]
    x = rows_ref[:, :448]
    width = own_ref.shape[1]
    step = 768
    for i, w_ref in enumerate((own_ref, other_ref)):
        for j in range(0, width, step):
            at = i * width + j
            o_ref[:, at : at + step] = mm(x, w_ref[:, j : j + step]).astype(BF)
    o_ref[:, 2 * width :] = rows_ref[:, 384:]


def half_body(p_ref, o_ref):
    width = o_ref.shape[1] - 128
    step = width // 6
    for j in range(0, width, step):
        part = p_ref[:, :, j : j + step].astype(F32)
        o_ref[:, j : j + step] = jnp.sum(part, axis=0).astype(BF)
    tail = jnp.sum(p_ref[:, :, width:].astype(F32), axis=0)
    lane = iota(tail.shape, 1)
    tail = jnp.where((lane == 64) | (lane == 65), tail, 0.0)
    squares = jnp.sum(tail, axis=1, keepdims=True)
    high = squares.astype(BF).astype(F32)
    tail = jnp.where(lane == 64, high, jnp.where(lane == 65, squares - high, 0.0))
    o_ref[:, width:] = tail.astype(BF)


def gate_body(p_ref, o_ref):
    units = o_ref.shape[2] // 2
    tail = jnp.sum(p_ref[:, :, 4 * units :].astype(F32), axis=0)
    lane = iota(tail.shape, 1)
    tail = jnp.where((lane == 64) | (lane == 65), tail, 0.0)
    factor = lax.rsqrt(jnp.sum(tail, axis=1, keepdims=True) / D + 1e-06)
    step = 384
    for i in range(2):
        for j in range(0, units, step):
            at = 2 * i * units + j
            gate = jnp.sum(p_ref[:, :, at : at + step].astype(F32), axis=0) * factor
            at = at + units
            up = jnp.sum(p_ref[:, :, at : at + step].astype(F32), axis=0) * factor
            hidden = (gate / (1.0 + jnp.exp(-gate)) * up).astype(BF)
            at = i * units + j
            for r in range(16):
                o_ref[r, :, at : at + step] = hidden


def local(
    queries,
    latent_cache,
    lengths,
    counts,
    residual,
    value_up,
    out_proj,
    norm_gain,
    gate_up,
    down_proj,
):
    shape = jax.ShapeDtypeStruct
    core = lax.axis_index("c").reshape(1)
    out_proj = out_proj.T
    down_proj = down_proj.T
    own = (value_up, out_proj, gate_up, down_proj)
    other = [lax.ppermute(w, "c", [(0, 1), (1, 0)]) for w in own]
    attended = call(
        attend_body,
        shape((8, 2, 16, KL), BF),
        lengths,
        counts,
        jnp.swapaxes(queries, 1, 2),
        jnp.swapaxes(latent_cache, 1, 2),
        any_space=4,
        scratch=[
            pltpu.SMEM((2,), jnp.int32),
            pltpu.SMEM((1,), jnp.int32),
            pltpu.VMEM((2, 576, 128), BF),
            pltpu.VMEM((2, 576, 512), BF),
            pltpu.SemaphoreType.DMA((6,)),
        ],
        limit=60,
    )
    received = exchange(attended, "z").reshape(256, KL)
    other[2] = other[2].reshape(other[2].shape[0], -1)
    gate_up = gate_up.reshape(gate_up.shape[0], -1)
    received, gate_up, other = lax.optimization_barrier((received, gate_up, other))
    own = (value_up, out_proj, gate_up, down_proj)
    value_up, out_proj, gate_up, down_proj = zip(own, other)
    values = call(value_body, shape((256, 2048), BF), core, received, *value_up, smem=1)
    values = exchange(values.reshape(16, 16, 2048), GRP).reshape(256, 2048)
    feats = residual.shape[1]
    partial = call(out_body, shape((256, feats), BF), values, *out_proj)
    pieces = exchange(partial.reshape(16, 16, feats), TP).reshape(256, feats)
    mine = lax.dynamic_slice_in_dim(residual, lax.axis_index(TP) * 32, 32, 0)
    combined, packed = call(
        mix_body,
        (shape((32, feats), F32), shape((8, 32, 512), BF)),
        pieces,
        mine,
        norm_gain.reshape(1, feats),
    )
    packed = exchange(packed, "z").reshape(256, 512)
    units = gate_up[0].shape[1] // 2
    terms = call(
        units_body,
        shape((256, 4 * units + 128), BF),
        core,
        packed,
        *gate_up,
        smem=1,
        scratch=[pltpu.VMEM((256, 512), BF)],
    )
    terms = exchange(terms.reshape(4, 64, -1), XYC, FIRST)
    terms = call(half_body, shape(terms.shape[1:], BF), terms)
    terms = exchange(terms.reshape(4, 16, -1), XYC, SECOND)
    hidden = call(gate_body, shape((16, 16, 2 * units), BF), terms)
    hidden = exchange(hidden, GRP).reshape(256, 2 * units)
    last = call(out_body, shape((256, feats), BF), hidden, *down_proj)
    last = exchange(last.reshape(8, 32, feats), "z")
    return (combined + jnp.sum(last.astype(F32), axis=0)).astype(BF)


def solution(mesh):
    inner = Mesh(mesh.devices.reshape(4, 4, 8, 2), GRP + TP)
    every = GRP + TP
    placed = (
        P(every, None, None),
        P(every, None, None),
        P(every),
        P(every),
        P(None, GRP),
        P(TP, None, None),
        P(TP, GRP),
        P(GRP),
        P(GRP, None, TP),
        P(TP, GRP),
    )
    return jax.shard_map(
        local, mesh=inner, in_specs=placed, out_specs=P(TP, GRP), check_vma=False
    )
```

```python
import jax
import jax.numpy as jnp
from jax import lax
from jax.experimental import pallas as pl
from jax.experimental.pallas import tpu as pltpu
from jax.sharding import Mesh, PartitionSpec as P

D = 7168
KL = 512
QKD = 192
GRP = ("y", "x")
TP = ("z", "c")
XYC = ("y", "x", "c")
LINES_X = [[[8 * y + 2 * x + c for x in range(4)] for y in range(4)] for c in range(2)]
LINES_Y = [[[8 * y + 2 * x + c for y in range(4)] for x in range(4)] for c in range(2)]
FIRST = LINES_X[0] + LINES_Y[1]
SECOND = LINES_Y[0] + LINES_X[1]
BF = jnp.bfloat16
F32 = jnp.float32


def exchange(parts, axes, groups=None):
    return lax.all_to_all(
        parts, axes, split_axis=0, concat_axis=0, axis_index_groups=groups
    )


def call(body, shapes, *args, smem=0, any_space=0, scratch=(), limit=8, flops=500000000):
    arrays = jax.tree.leaves((args, shapes))
    size = sum(a.size * a.dtype.itemsize for a in arrays)
    cost = pl.CostEstimate(flops=flops, bytes_accessed=size, transcendentals=0)
    cost = cost if flops else None
    spaces = [pltpu.SMEM] * smem + [pltpu.HBM] * any_space
    spaces = spaces + [pltpu.VMEM] * (len(args) - len(spaces))
    return pl.pallas_call(
        body,
        out_shape=shapes,
        in_specs=[pl.BlockSpec(memory_space=space) for space in spaces],
        scratch_shapes=scratch,
        cost_estimate=cost,
        compiler_params=pltpu.CompilerParams(vmem_limit_bytes=limit * 2**20),
    )(*args)


def iota(shape, dim):
    return lax.broadcasted_iota(jnp.int32, shape, dim)


def mm(a, b):
    return jnp.dot(a, b, preferred_element_type=F32)


def mm_t(a, b):
    return lax.dot_general(a, b, (((1,), (1,)), ((), ())), preferred_element_type=F32)


def attend_body(len_hbm, cnt_hbm, q_hbm, c_hbm, o_ref, lengths, counts, q_ref, c_ref, sems):
    copies = [
        pltpu.make_async_copy(len_hbm, lengths, sems.at[0]),
        pltpu.make_async_copy(cnt_hbm, counts, sems.at[1]),
    ]
    for slot in range(2):
        copies.append(
            pltpu.make_async_copy(q_hbm.at[slot], q_ref.at[slot], sems.at[2 + 2 * slot])
        )
        copies.append(
            pltpu.make_async_copy(c_hbm.at[slot], c_ref.at[slot], sems.at[3 + 2 * slot])
        )
    for copy in copies:
        copy.start()
    copies[0].wait()
    copies[1].wait()
    for slot in range(2):
        copies[2 + 2 * slot].wait()
        query = q_ref[slot].T
        copies[3 + 2 * slot].wait()
        scores = mm(query, c_ref[slot]) * QKD ** (-0.5)
        scores = jnp.where(iota(scores.shape, 1) < lengths[slot], scores, -jnp.inf)
        expo = jnp.exp(scores - jnp.max(scores, axis=1, keepdims=True))
        scale = 1.0 / jnp.sum(expo, axis=1, keepdims=True)
        summed = mm_t(expo.astype(BF), c_ref[slot, :KL, :])
        summed = jnp.where(slot < counts[0], summed * scale, 0.0)
        o_ref[:, slot] = summed.astype(BF).reshape(8, 16, KL)


def value_body(core, x_ref, own_ref, other_ref, o_ref):
    at = iota((256, 256), 0)
    source = (at & 15) * 16 + ((at >> 4) ^ (8 * core[0]))
    pick = (iota((256, 256), 1) == source).astype(BF)
    x = mm(pick, x_ref[...]).astype(BF)
    for i, w_ref in enumerate((own_ref, other_ref)):
        for h in range(8):
            k = 8 * i + h
            value = mm(x[16 * k : 16 * k + 16], w_ref[h]).astype(BF)
            for r in range(16):
                o_ref[16 * r : 16 * r + 16, 128 * k : 128 * k + 128] = value


def out_body(v_ref, own_ref, other_ref, o_ref):
    depth = own_ref.shape[1]
    total = mm_t(v_ref[:, :depth], own_ref[...])
    total = total + mm_t(v_ref[:, depth:], other_ref[...])
    o_ref[...] = total.astype(BF)


def mix_body(p_ref, mine_ref, gain_ref, c_ref, o_ref):
    k = iota((32, 256), 1)
    place = ((k >> 1) & 7) * 4 + ((k >> 4) & 1) * 2 + (k & 1)
    pick = (iota((32, 256), 0) == place).astype(BF)
    combined = mine_ref[...].astype(F32) + mm(pick, p_ref[...])
    c_ref[...] = combined
    squares = jnp.sum(combined * combined, axis=1, keepdims=True)
    high = squares.astype(BF).astype(F32)
    lane = iota((32, 512), 1)
    extra = jnp.where(lane == 448, high, jnp.where(lane == 449, squares - high, 0.0))
    extra = extra.astype(BF)
    scaled = (combined * gain_ref[...].astype(F32)).astype(BF)
    for z in range(8):
        o_ref[z] = extra
        o_ref[z, :, :448] = scaled


def units_body(core, x_ref, own_ref, other_ref, o_ref, rows_ref):
    for i in range(4):
        for j in range(4):
            block = jnp.where(core[0] == 0, 4 * j + i, 4 * i + j)
            at = pl.multiple_of(block * 16, 16)
            to = 16 * (4 * i + j)
            rows_ref[to : to + 16] = x_ref[pl.ds(at, 16)]
    x = rows_ref[:, :448]
    width = own_ref.shape[1]
    step = 768
    for i, w_ref in enumerate((own_ref, other_ref)):
        for j in range(0, width, step):
            at = i * width + j
            o_ref[:, at : at + step] = mm(x, w_ref[:, j : j + step]).astype(BF)
    o_ref[:, 2 * width :] = rows_ref[:, 384:]


def half_body(p_ref, o_ref):
    width = o_ref.shape[1] - 128
    step = width // 6
    for j in range(0, width, step):
        part = p_ref[:, :, j : j + step].astype(F32)
        o_ref[:, j : j + step] = jnp.sum(part, axis=0).astype(BF)
    tail = jnp.sum(p_ref[:, :, width:].astype(F32), axis=0)
    lane = iota(tail.shape, 1)
    tail = jnp.where((lane == 64) | (lane == 65), tail, 0.0)
    squares = jnp.sum(tail, axis=1, keepdims=True)
    high = squares.astype(BF).astype(F32)
    tail = jnp.where(lane == 64, high, jnp.where(lane == 65, squares - high, 0.0))
    o_ref[:, width:] = tail.astype(BF)


def gate_body(p_ref, o_ref):
    units = o_ref.shape[2] // 2
    tail = jnp.sum(p_ref[:, :, 4 * units :].astype(F32), axis=0)
    lane = iota(tail.shape, 1)
    tail = jnp.where((lane == 64) | (lane == 65), tail, 0.0)
    factor = lax.rsqrt(jnp.sum(tail, axis=1, keepdims=True) / D + 1e-06)
    step = 384
    for i in range(2):
        for j in range(0, units, step):
            at = 2 * i * units + j
            gate = jnp.sum(p_ref[:, :, at : at + step].astype(F32), axis=0) * factor
            at = at + units
            up = jnp.sum(p_ref[:, :, at : at + step].astype(F32), axis=0) * factor
            hidden = (gate / (1.0 + jnp.exp(-gate)) * up).astype(BF)
            at = i * units + j
            for r in range(16):
                o_ref[r, :, at : at + step] = hidden


def last_body(c_ref, p_ref, o_ref):
    o_ref[...] = (c_ref[...] + jnp.sum(p_ref[...].astype(F32), axis=0)).astype(BF)


def local(
    queries,
    latent_cache,
    lengths,
    counts,
    residual,
    value_up,
    out_proj,
    norm_gain,
    gate_up,
    down_proj,
):
    shape = jax.ShapeDtypeStruct
    core = lax.axis_index("c").reshape(1)
    out_proj = out_proj.T
    down_proj = down_proj.T
    own = (value_up, out_proj, gate_up, down_proj)
    other = [lax.ppermute(w, "c", [(0, 1), (1, 0)]) for w in own]
    attended = call(
        attend_body,
        shape((8, 2, 16, KL), BF),
        lengths,
        counts,
        jnp.swapaxes(queries, 1, 2),
        jnp.swapaxes(latent_cache, 1, 2),
        any_space=4,
        scratch=[
            pltpu.SMEM((2,), jnp.int32),
            pltpu.SMEM((1,), jnp.int32),
            pltpu.VMEM((2, 576, 128), BF),
            pltpu.VMEM((2, 576, 512), BF),
            pltpu.SemaphoreType.DMA((6,)),
        ],
        limit=60,
    )
    received = exchange(attended, "z").reshape(256, KL)
    other[2] = other[2].reshape(other[2].shape[0], -1)
    gate_up = gate_up.reshape(gate_up.shape[0], -1)
    mine = lax.dynamic_slice_in_dim(residual, lax.axis_index(TP) * 32, 32, 0)
    gain = norm_gain.reshape(1, -1)
    received, gate_up, other, mine, gain = lax.optimization_barrier(
        (received, gate_up, other, mine, gain)
    )
    own = (value_up, out_proj, gate_up, down_proj)
    value_up, out_proj, gate_up, down_proj = zip(own, other)
    values = call(
        value_body,
        shape((256, 2048), BF),
        core,
        received,
        *value_up,
        smem=1,
        flops=0,
    )
    values = exchange(values.reshape(16, 16, 2048), GRP).reshape(256, 2048)
    feats = residual.shape[1]
    partial = call(out_body, shape((256, feats), BF), values, *out_proj)
    pieces = exchange(partial.reshape(16, 16, feats), TP).reshape(256, feats)
    combined, packed = call(
        mix_body,
        (shape((32, feats), F32), shape((8, 32, 512), BF)),
        pieces,
        mine,
        gain,
    )
    packed = exchange(packed, "z").reshape(256, 512)
    units = gate_up[0].shape[1] // 2
    terms = call(
        units_body,
        shape((256, 4 * units + 128), BF),
        core,
        packed,
        *gate_up,
        smem=1,
        scratch=[pltpu.VMEM((256, 512), BF)],
    )
    terms = exchange(terms.reshape(4, 64, -1), XYC, FIRST)
    terms = call(half_body, shape(terms.shape[1:], BF), terms)
    terms = exchange(terms.reshape(4, 16, -1), XYC, SECOND)
    hidden = call(gate_body, shape((16, 16, 2 * units), BF), terms)
    hidden = exchange(hidden, GRP).reshape(256, 2 * units)
    last = call(out_body, shape((256, feats), BF), hidden, *down_proj)
    last = exchange(last.reshape(8, 32, feats), "z")
    return call(last_body, shape((32, feats), BF), combined, last)


def solution(mesh):
    inner = Mesh(mesh.devices.reshape(4, 4, 8, 2), GRP + TP)
    every = GRP + TP
    placed = (
        P(every, None, None),
        P(every, None, None),
        P(every),
        P(every),
        P(None, GRP),
        P(TP, None, None),
        P(TP, GRP),
        P(GRP),
        P(GRP, None, TP),
        P(TP, GRP),
    )
    return jax.shard_map(
        local, mesh=inner, in_specs=placed, out_specs=P(TP, GRP), check_vma=False
    )
```

```python
import jax
import jax.numpy as jnp
from jax import lax
from jax.experimental import pallas as pl
from jax.experimental.pallas import tpu as pltpu
from jax.sharding import Mesh, PartitionSpec as P

D = 7168
KL = 512
QKD = 192
GRP = ("y", "x")
TP = ("z", "c")
XYC = ("y", "x", "c")
LINES_X = [[[8 * y + 2 * x + c for x in range(4)] for y in range(4)] for c in range(2)]
LINES_Y = [[[8 * y + 2 * x + c for y in range(4)] for x in range(4)] for c in range(2)]
FIRST = LINES_X[0] + LINES_Y[1]
SECOND = LINES_Y[0] + LINES_X[1]
BF = jnp.bfloat16
F32 = jnp.float32


def exchange(parts, axes, groups=None):
    return lax.all_to_all(
        parts, axes, split_axis=0, concat_axis=0, axis_index_groups=groups
    )


def call(body, shapes, *args, smem=0, any_space=0, scratch=(), limit=8, flops=500000000):
    arrays = jax.tree.leaves((args, shapes))
    size = sum(a.size * a.dtype.itemsize for a in arrays)
    cost = pl.CostEstimate(flops=flops, bytes_accessed=size, transcendentals=0)
    cost = cost if flops else None
    spaces = [pltpu.SMEM] * smem + [pltpu.HBM] * any_space
    spaces = spaces + [pltpu.VMEM] * (len(args) - len(spaces))
    return pl.pallas_call(
        body,
        out_shape=shapes,
        in_specs=[pl.BlockSpec(memory_space=space) for space in spaces],
        scratch_shapes=scratch,
        cost_estimate=cost,
        compiler_params=pltpu.CompilerParams(vmem_limit_bytes=limit * 2**20),
    )(*args)


def iota(shape, dim):
    return lax.broadcasted_iota(jnp.int32, shape, dim)


def mm(a, b):
    return jnp.dot(a, b, preferred_element_type=F32)


def mm_t(a, b):
    return lax.dot_general(a, b, (((1,), (1,)), ((), ())), preferred_element_type=F32)


def attend_body(len_hbm, cnt_hbm, q_hbm, c_hbm, o_ref, lengths, counts, q_ref, c_ref, sems):
    copies = [
        pltpu.make_async_copy(len_hbm, lengths, sems.at[0]),
        pltpu.make_async_copy(cnt_hbm, counts, sems.at[1]),
    ]
    for slot in range(2):
        copies.append(
            pltpu.make_async_copy(q_hbm.at[slot], q_ref.at[slot], sems.at[2 + 2 * slot])
        )
        copies.append(
            pltpu.make_async_copy(c_hbm.at[slot], c_ref.at[slot], sems.at[3 + 2 * slot])
        )
    for copy in copies:
        copy.start()
    copies[0].wait()
    copies[1].wait()
    for slot in range(2):
        copies[2 + 2 * slot].wait()
        query = q_ref[slot].T
        copies[3 + 2 * slot].wait()
        scores = mm(query, c_ref[slot]) * QKD ** (-0.5)
        scores = jnp.where(iota(scores.shape, 1) < lengths[slot], scores, -jnp.inf)
        expo = jnp.exp(scores - jnp.max(scores, axis=1, keepdims=True))
        scale = 1.0 / jnp.sum(expo, axis=1, keepdims=True)
        summed = mm_t(expo.astype(BF), c_ref[slot, :KL, :])
        summed = jnp.where(slot < counts[0], summed * scale, 0.0)
        o_ref[:, slot] = summed.astype(BF).reshape(8, 16, KL)


def value_body(core, x_ref, own_ref, other_ref, o_ref):
    at = iota((256, 256), 0)
    source = (at & 15) * 16 + ((at >> 4) ^ (8 * core[0]))
    pick = (iota((256, 256), 1) == source).astype(BF)
    x = mm(pick, x_ref[...]).astype(BF)
    for i, w_ref in enumerate((own_ref, other_ref)):
        for h in range(8):
            k = 8 * i + h
            value = mm(x[16 * k : 16 * k + 16], w_ref[h]).astype(BF)
            for r in range(16):
                o_ref[16 * r : 16 * r + 16, 128 * k : 128 * k + 128] = value


def out_body(v_ref, own_ref, other_ref, o_ref):
    depth = own_ref.shape[1]
    total = mm_t(v_ref[:, :depth], own_ref[...])
    total = total + mm_t(v_ref[:, depth:], other_ref[...])
    o_ref[...] = total.astype(BF)


def mix_body(p_ref, mine_ref, gain_ref, c_ref, o_ref):
    k = iota((32, 256), 1)
    place = ((k >> 1) & 7) * 4 + ((k >> 4) & 1) * 2 + (k & 1)
    pick = (iota((32, 256), 0) == place).astype(BF)
    combined = mine_ref[...].astype(F32) + mm(pick, p_ref[...])
    c_ref[...] = combined
    squares = jnp.sum(combined * combined, axis=1, keepdims=True)
    high = squares.astype(BF).astype(F32)
    lane = iota((32, 512), 1)
    extra = jnp.where(lane == 448, high, jnp.where(lane == 449, squares - high, 0.0))
    extra = extra.astype(BF)
    scaled = (combined * gain_ref[...].astype(F32)).astype(BF)
    for z in range(8):
        o_ref[z] = extra
        o_ref[z, :, :448] = scaled


def units_body(core, x_ref, own_ref, other_ref, o_ref, rows_ref):
    for i in range(4):
        for j in range(4):
            block = jnp.where(core[0] == 0, 4 * j + i, 4 * i + j)
            at = pl.multiple_of(block * 16, 16)
            to = 16 * (4 * i + j)
            rows_ref[to : to + 16] = x_ref[pl.ds(at, 16)]
    x = rows_ref[:, :448]
    width = own_ref.shape[1]
    step = 768
    for i, w_ref in enumerate((own_ref, other_ref)):
        for j in range(0, width, step):
            at = i * width + j
            o_ref[:, at : at + step] = mm(x, w_ref[:, j : j + step]).astype(BF)
    o_ref[:, 2 * width :] = rows_ref[:, 384:]


def half_body(p_ref, o_ref):
    width = o_ref.shape[1] - 128
    step = width // 6
    for j in range(0, width, step):
        part = p_ref[:, :, j : j + step].astype(F32)
        o_ref[:, j : j + step] = jnp.sum(part, axis=0).astype(BF)
    tail = jnp.sum(p_ref[:, :, width:].astype(F32), axis=0)
    lane = iota(tail.shape, 1)
    tail = jnp.where((lane == 64) | (lane == 65), tail, 0.0)
    squares = jnp.sum(tail, axis=1, keepdims=True)
    high = squares.astype(BF).astype(F32)
    tail = jnp.where(lane == 64, high, jnp.where(lane == 65, squares - high, 0.0))
    o_ref[:, width:] = tail.astype(BF)


def gate_body(p_ref, o_ref):
    units = o_ref.shape[2] // 2
    tail = jnp.sum(p_ref[:, :, 4 * units :].astype(F32), axis=0)
    lane = iota(tail.shape, 1)
    tail = jnp.where((lane == 64) | (lane == 65), tail, 0.0)
    factor = lax.rsqrt(jnp.sum(tail, axis=1, keepdims=True) / D + 1e-06)
    step = 384
    for i in range(2):
        for j in range(0, units, step):
            at = 2 * i * units + j
            gate = jnp.sum(p_ref[:, :, at : at + step].astype(F32), axis=0) * factor
            at = at + units
            up = jnp.sum(p_ref[:, :, at : at + step].astype(F32), axis=0) * factor
            hidden = (gate / (1.0 + jnp.exp(-gate)) * up).astype(BF)
            at = i * units + j
            for r in range(16):
                o_ref[r, :, at : at + step] = hidden


def last_body(c_ref, p_ref, o_ref):
    o_ref[...] = (c_ref[...] + jnp.sum(p_ref[...].astype(F32), axis=0)).astype(BF)


def local(
    queries,
    latent_cache,
    lengths,
    counts,
    residual,
    value_up,
    out_proj,
    norm_gain,
    gate_up,
    down_proj,
):
    shape = jax.ShapeDtypeStruct
    core = lax.axis_index("c").reshape(1)
    out_proj = out_proj.T
    down_proj = down_proj.T
    own = (value_up, out_proj, gate_up, down_proj)
    other = [lax.ppermute(w, "c", [(0, 1), (1, 0)]) for w in own]
    attended = call(
        attend_body,
        shape((8, 2, 16, KL), BF),
        lengths,
        counts,
        jnp.swapaxes(queries, 1, 2),
        jnp.swapaxes(latent_cache, 1, 2),
        any_space=4,
        scratch=[
            pltpu.SMEM((2,), jnp.int32),
            pltpu.SMEM((1,), jnp.int32),
            pltpu.VMEM((2, 576, 128), BF),
            pltpu.VMEM((2, 576, 512), BF),
            pltpu.SemaphoreType.DMA((6,)),
        ],
        limit=60,
    )
    received = exchange(attended, "z").reshape(256, KL)
    one = (core[0] < 2).astype(BF)
    other = [other[0], other[1] * one, other[2], other[3] * one]
    other[2] = other[2].reshape(other[2].shape[0], -1)
    gate_up = gate_up.reshape(gate_up.shape[0], -1)
    mine = lax.dynamic_slice_in_dim(residual, lax.axis_index(TP) * 32, 32, 0)
    gain = norm_gain.reshape(1, -1)
    received, gate_up, other, mine, gain = lax.optimization_barrier(
        (received, gate_up, other, mine, gain)
    )
    own = (value_up, out_proj, gate_up, down_proj)
    value_up, out_proj, gate_up, down_proj = zip(own, other)
    values = call(
        value_body,
        shape((256, 2048), BF),
        core,
        received,
        *value_up,
        smem=1,
        flops=0,
    )
    values = exchange(values.reshape(16, 16, 2048), GRP).reshape(256, 2048)
    feats = residual.shape[1]
    partial = call(out_body, shape((256, feats), BF), values, *out_proj)
    pieces = exchange(partial.reshape(16, 16, feats), TP).reshape(256, feats)
    combined, packed = call(
        mix_body,
        (shape((32, feats), F32), shape((8, 32, 512), BF)),
        pieces,
        mine,
        gain,
    )
    packed = exchange(packed, "z").reshape(256, 512)
    units = gate_up[0].shape[1] // 2
    terms = call(
        units_body,
        shape((256, 4 * units + 128), BF),
        core,
        packed,
        *gate_up,
        smem=1,
        scratch=[pltpu.VMEM((256, 512), BF)],
    )
    terms = exchange(terms.reshape(4, 64, -1), XYC, FIRST)
    terms = call(half_body, shape(terms.shape[1:], BF), terms)
    terms = exchange(terms.reshape(4, 16, -1), XYC, SECOND)
    hidden = call(gate_body, shape((16, 16, 2 * units), BF), terms)
    hidden = exchange(hidden, GRP).reshape(256, 2 * units)
    last = call(out_body, shape((256, feats), BF), hidden, *down_proj)
    last = exchange(last.reshape(8, 32, feats), "z")
    return call(last_body, shape((32, feats), BF), combined, last)


def solution(mesh):
    inner = Mesh(mesh.devices.reshape(4, 4, 8, 2), GRP + TP)
    every = GRP + TP
    placed = (
        P(every, None, None),
        P(every, None, None),
        P(every),
        P(every),
        P(None, GRP),
        P(TP, None, None),
        P(TP, GRP),
        P(GRP),
        P(GRP, None, TP),
        P(TP, GRP),
    )
    return jax.shard_map(
        local, mesh=inner, in_specs=placed, out_specs=P(TP, GRP), check_vma=False
    )
```
